32 devices in a mesh: harm: 4 (over z), node: 8 (over y, x, core).
Axes of the slice: x: 2, y: 2, z: 4, core: 2. Of those that a mesh axis runs over, the one named last changes fastest.
Arguments:
- adjoint: bfloat16 [128, 4, 32768], P('harm', None, 'node'), may hold values from -6 to 6
- source: float32 [128, 131072], P(None, ('harm', 'node')), may hold values from -6 to 6
- rad_coeff: bfloat16 [128, 131072], P(None, ('harm', 'node')), may hold values from 0.19921875 to 2
- capacity: float32 [131072], P(('harm', 'node')), may hold values from 0.005 to 0.03
- inv_diag: float32 [131072], P(('harm', 'node')), may hold values from 0.1 to 0.5
- blocks: bfloat16 [1024, 4, 128, 128], P(('harm', 'node')), may hold values from -0.25 to 0.25
- block_cols: int32 [1024, 4], P(('harm', 'node')), may hold values from 0 to 1023, as said below
- zone_of: int32 [131072], P(('harm', 'node')), may hold values from 0 to 1279, as said below
- heater_weight: float32 [131072], P(('harm', 'node')), may hold values from 0.2 to 2
Outputs:
- updated: bfloat16 [128, 4, 32768], P('harm', None, 'node')
- gradient: float32 [1280, 128], P(('harm', 'node'))
The draws below stay inside these ranges and needn't reach their ends.
Inputs may be any that keep to these rules, and one draw needn't show every extreme that they name: `block_cols`: with d = b // 32 and D = 32: slot 0 of row block b names b itself; slot 1 lies in row blocks max(d - 1, 0) * 32 to (max(d - 1, 0) + 1) * 32 - 1; slot 2 in min(d + 1, D - 1) * 32 to (min(d + 1, D - 1) + 1) * 32 - 1; the other slots in (d - 1) * 32 to (d + 2) * 32 - 1. `zone_of`: node n lies in a zone z with (n // 4096 - 1) * 40 <= z < (n // 4096 + 2) * 40.
All inputs are finite; a program needn't handle non-finite values.
Results may differ from the reference program's by a relative error of at most 0.0035.
Values may be sent and summed in bfloat16 or wider, within the bound.
A program may use at most 64 MiB of HBM per device.

```python
import math
import jax
import jax.numpy as jnp
from jax import lax

K = 128
P_SIZE = 128
BLK = 128
NNZ = 4
SUB = 4096
ZONE_DEV = 40
NODES = 131072
NBLK = 1024
RB = 32
ZONES = 1280
N_HARM = 4
N_NODE = 8


def draw_block_cols(key, part):
    key_low = jax.random.fold_in(key, 21)
    key_high = jax.random.fold_in(key, 22)
    key_rest = jax.random.fold_in(key, 23)
    row_device = jnp.arange(NBLK, dtype=jnp.int32) // RB
    device_total = NBLK // RB
    lower = jnp.maximum(row_device - 1, 0) * RB
    upper = jnp.minimum(row_device + 2, device_total) * RB
    low_dev = jnp.maximum(row_device - 1, 0)
    high_dev = jnp.minimum(row_device + 1, device_total - 1)
    low_pick = low_dev * RB + jax.random.randint(key_low, (NBLK,), 0, RB, dtype=jnp.int32)
    high_pick = high_dev * RB + jax.random.randint(key_high, (NBLK,), 0, RB, dtype=jnp.int32)
    picked = jax.random.randint(key_rest, (NBLK, NNZ), lower[:, None], upper[:, None], dtype=jnp.int32)
    picked = picked.at[:, 0].set(jnp.arange(NBLK, dtype=jnp.int32))
    picked = picked.at[:, 1].set(low_pick)
    picked = picked.at[:, 2].set(high_pick)
    return picked.astype(jnp.int32)


def draw_zone_of(key, part):
    key_spill = jax.random.fold_in(key, 11)
    key_side = jax.random.fold_in(key, 12)
    key_pick = jax.random.fold_in(key, 13)
    node_index = jnp.arange(NODES, dtype=jnp.int32)
    device_total = NODES // SUB
    owner = node_index // SUB
    inside = node_index % SUB
    home_zone = owner * ZONE_DEV + inside * ZONE_DEV // SUB
    spilled = jax.random.randint(key_spill, (NODES,), 0, 4, dtype=jnp.int32) == 0
    side_step = jax.random.randint(key_side, (NODES,), 0, 2, dtype=jnp.int32) * 2 - 1
    target = owner + side_step
    usable = (target >= 0) & (target < device_total)
    other_zone = target * ZONE_DEV + jax.random.randint(key_pick, (NODES,), 0, ZONE_DEV, dtype=jnp.int32)
    return jnp.where(spilled & usable, other_zone, home_zone).astype(jnp.int32)


def shard_levels(stream_key, shape, cuts, low, high):
    loudness = 1.0
    for position, shards_of in cuts:
        steps = jax.random.uniform(jax.random.fold_in(jax.random.fold_in(stream_key, 6), position), (shards_of,), jnp.float32, low / len(cuts), high / len(cuts))
        loudness = loudness * jnp.repeat(jnp.exp(steps), shape[position] // shards_of).reshape((-1,) + (1,) * (len(shape) - 1 - position))
    return loudness


def noise(key, dims, width, limit, shards=(), kind=jnp.bfloat16):
    factor_of = shard_levels(key, dims, shards, -0.22, 0.18) if shards else 1.0
    result = jax.random.normal(key, dims, jnp.float32) * width * factor_of
    return jnp.minimum(jnp.maximum(result, -limit), limit).astype(kind)


def setup_inputs(seed: int = 0) -> dict:
    keys = jax.random.split(jax.random.key(seed), 10)
    return {
        "adjoint": noise(keys[0], (K, N_HARM, N_NODE * SUB), 1.0, 6.0, ((0, 4), (2, 8))),
        "source": noise(keys[1], (K, NODES), 1.0, 6.0, ((1, 32),), jnp.float32),
        "rad_coeff": jnp.clip(jnp.exp(math.log(2.0) - 2.306499 * jax.random.uniform(keys[2], (P_SIZE, NODES), jnp.float32) ** shard_levels(keys[2], (P_SIZE, NODES), ((1, 32),), -0.2, 0.2)), 0.19921875, 2.0).astype(jnp.bfloat16),
        "capacity": jnp.clip(jnp.exp(math.log(0.03) - 1.7917595 * jax.random.uniform(keys[3], (NODES,), jnp.float32) ** shard_levels(keys[3], (NODES,), ((0, 32),), -0.2, 0.2)), 0.005, 0.03),
        "inv_diag": jnp.clip(jnp.exp(math.log(0.5) - 1.609438 * jax.random.uniform(keys[4], (NODES,), jnp.float32) ** shard_levels(keys[4], (NODES,), ((0, 32),), -0.2, 0.2)), 0.1, 0.5),
        "blocks": noise(keys[5], (NBLK, NNZ, BLK, BLK), (BLK * NNZ) ** -0.5, 0.25, ((0, 32),)),
        "block_cols": draw_block_cols(jax.random.fold_in(keys[9], 71), 0),
        "zone_of": draw_zone_of(jax.random.fold_in(keys[9], 71), 0),
        "heater_weight": jnp.clip(jnp.exp(math.log(2.0) - 2.3025851 * jax.random.uniform(keys[8], (NODES,), jnp.float32) ** shard_levels(keys[8], (NODES,), ((0, 32),), -0.2, 0.2)), 0.2, 2.0),
    }


def fourier_basis(count):
    sample_index = jnp.arange(count, dtype=jnp.float32)[:, None]
    column_index = jnp.arange(count)[None, :]
    half_count = count // 2
    frequency = jnp.where(column_index <= half_count, column_index, column_index - half_count).astype(jnp.float32)
    angle = 2.0 * math.pi * frequency * sample_index / count
    values_table = jnp.where(column_index <= half_count, jnp.cos(angle), jnp.sin(angle))
    scaling = jnp.where((column_index == 0) | (column_index == half_count), math.sqrt(1.0 / count), math.sqrt(2.0 / count))
    return (values_table * scaling).astype(jnp.bfloat16)

def derivative_term(field):
    half_count = field.shape[0] // 2
    wave_number = jnp.arange(1, half_count, dtype=jnp.float32)[:, None]
    zero_row = jnp.zeros((1, field.shape[1]), jnp.float32)
    upper_rows = wave_number * field[half_count + 1:]
    lower_rows = -wave_number * field[1:half_count]
    return jnp.concatenate([zero_row, upper_rows, zero_row, lower_rows], axis=0)

def reference(adjoint, source, rad_coeff, capacity, inv_diag, blocks, block_cols, zone_of, heater_weight):
    adjoint_nodes = adjoint.reshape(K, NODES)
    fourier = fourier_basis(K)
    lam_blocks = adjoint_nodes.reshape(K, NBLK, BLK)
    groups = NODES // SUB

    def group_step(group):
        start = (group * SUB).astype(jnp.int32)
        field = lax.dynamic_slice_in_dim(adjoint_nodes, start, SUB, 1)
        samples = jnp.dot(fourier, field, preferred_element_type=jnp.float32)
        coeff_slice = lax.dynamic_slice_in_dim(rad_coeff, start, SUB, 1)
        weighted = (coeff_slice.astype(jnp.float32) * samples).astype(jnp.bfloat16)
        radiative = jnp.dot(fourier.T, weighted, preferred_element_type=jnp.float32)
        rate_term = derivative_term(field.astype(jnp.float32))
        block_start = (group * RB).astype(jnp.int32)
        col_slice = lax.dynamic_slice_in_dim(block_cols, block_start, RB, 0)
        block_slice = lax.dynamic_slice_in_dim(blocks, block_start, RB, 0)
        gathered = jnp.take(lam_blocks, col_slice, axis=1)
        conduction = jnp.einsum('kbsj,bsij->kbi', gathered.astype(jnp.float32), block_slice.astype(jnp.float32)).reshape(K, SUB)
        source_slice = lax.dynamic_slice_in_dim(source, start, SUB, 1)
        capacity_slice = lax.dynamic_slice_in_dim(capacity, start, SUB, 0)
        inverse_slice = lax.dynamic_slice_in_dim(inv_diag, start, SUB, 0)
        residual = source_slice - (capacity_slice[None, :] * rate_term + conduction + radiative)
        return (field.astype(jnp.float32) + inverse_slice[None, :] * residual).astype(jnp.bfloat16)
    pieces = lax.map(group_step, jnp.arange(groups, dtype=jnp.int32))
    updated_nodes = jnp.transpose(pieces, (1, 0, 2)).reshape(K, NODES)
    weighted_terms = (updated_nodes.astype(jnp.float32) * heater_weight[None, :]).T
    gradient = jax.ops.segment_sum(weighted_terms, zone_of, num_segments=ZONES)
    return (updated_nodes.reshape(K, N_HARM, N_NODE * SUB), gradient)
```

```python
import functools
import math

import jax
import jax.numpy as jnp
import numpy as np
from jax import lax
from jax.experimental import pallas as pl
from jax.experimental.pallas import tpu as pltpu
from jax.sharding import PartitionSpec as P

ZONE_DEV = 40
ROWS = 16
GROUPS = 4
WIDTH = 256
MESH = pl.DeviceIdType.MESH
NT = (((1,), (1,)), ((), ()))


def fourier_basis(count):
    sample_index = np.arange(count, dtype=np.float32)[:, None]
    column_index = np.arange(count)[None, :]
    half_count = count // 2
    frequency = np.where(
        column_index <= half_count, column_index, column_index - half_count
    ).astype(np.float32)
    angle = np.float32(2.0 * math.pi) * frequency * sample_index / np.float32(count)
    values_table = np.where(column_index <= half_count, np.cos(angle), np.sin(angle))
    scaling = np.where(
        (column_index == 0) | (column_index == half_count),
        math.sqrt(1.0 / count),
        math.sqrt(2.0 / count),
    ).astype(np.float32)
    return (values_table * scaling).astype(jnp.bfloat16)


def kernel(
    n_harm,
    n_node,
    n_chunk,
    adj,
    src_any,
    rad_any,
    blk_any,
    capacity,
    inv_diag,
    weight,
    zone,
    cols,
    fourier,
    fourier_t,
    rate_k,
    ret,
    grad,
    *scratch,
):
    ext = scratch[:n_chunk]
    (
        src,
        rad,
        blk,
        upd,
        select,
        part,
        from_prev,
        from_next,
        load_sem,
        in_send,
        in_recv,
        halo_send,
        halo_recv,
        out_send,
        out_recv,
        own_sem,
        part_send,
        part_recv,
    ) = scratch[n_chunk:]
    row_blocks = adj.shape[2]
    nodes = row_blocks * 128
    chunk_rows = n_harm * ROWS
    me_h = lax.axis_index("harm")
    me_n = lax.axis_index("node")
    pos = me_h * n_node + me_n
    last = n_harm * n_node - 1
    has_prev = pos > 0
    has_next = pos < last
    prev = jnp.maximum(pos - 1, 0)
    following = jnp.minimum(pos + 1, last)
    prev_id = (prev // n_node, prev % n_node)
    next_id = (following // n_node, following % n_node)
    sides = ((has_prev, prev_id, 2), (has_next, next_id, 0))

    loads = [
        pltpu.make_async_copy(src_any, src, load_sem.at[0]),
        pltpu.make_async_copy(rad_any, rad, load_sem.at[1]),
        pltpu.make_async_copy(blk_any, blk, load_sem.at[2]),
    ]
    own = [
        pltpu.make_async_copy(
            adj.at[me_h, c], ext[c].at[me_h, pl.ds(row_blocks, row_blocks)], load_sem.at[3 + c]
        )
        for c in range(n_chunk)
    ]

    barrier = pltpu.get_barrier_semaphore()
    for d in range(1, n_harm):
        peer = lax.rem(me_h + d, n_harm)
        pl.semaphore_signal(barrier, inc=1, device_id=(peer, me_n), device_id_type=MESH)
    for there, device, _ in sides:

        @pl.when(there)
        def _(device=device):
            pl.semaphore_signal(barrier, inc=1, device_id=device, device_id_type=MESH)

    pl.semaphore_wait(
        barrier, n_harm - 1 + has_prev.astype(jnp.int32) + has_next.astype(jnp.int32)
    )

    def arrive(d, c):
        peer = lax.rem(me_h + d, n_harm)
        return pltpu.make_async_remote_copy(
            src_ref=adj.at[peer, c],
            dst_ref=ext[c].at[me_h, pl.ds(row_blocks, row_blocks)],
            send_sem=in_send.at[d, c],
            recv_sem=in_recv.at[d, c],
            device_id=(peer, me_n),
            device_id_type=MESH,
        )

    def halo(d, c, side):
        _, device, place = sides[side]
        piece = lax.rem(me_h - d + n_harm, n_harm)
        if d == 0:
            source = adj.at[me_h, c]
        else:
            source = ext[c].at[piece, pl.ds(row_blocks, row_blocks)]
        return pltpu.make_async_remote_copy(
            src_ref=source,
            dst_ref=ext[c].at[piece, pl.ds(place * row_blocks, row_blocks)],
            send_sem=halo_send.at[side, d, c],
            recv_sem=halo_recv.at[side, d, c],
            device_id=device,
            device_id_type=MESH,
        )

    def start_halo(d, c):
        for side in range(2):

            @pl.when(sides[side][0])
            def _(side=side):
                halo(d, c, side).start()

    for c in range(n_chunk):
        for d in range(1, n_harm):
            arrive(d, c).start()
        own[c].start()
        start_halo(0, c)
    for load in loads:
        load.start()

    zone_row = lax.broadcasted_iota(jnp.int32, (128, WIDTH), 0)

    def select_step(i, carry):
        at = pl.ds(pl.multiple_of(i * WIDTH, WIDTH), WIDTH)
        hit = zone_row == (zone[:, at] - (pos - 1) * ZONE_DEV)
        w = weight[:, at]
        high = w.astype(jnp.bfloat16).astype(jnp.float32)
        select[0:128, at] = jnp.where(hit, high, 0.0).astype(jnp.bfloat16)
        select[128:256, at] = jnp.where(hit, w - high, 0.0).astype(jnp.bfloat16)
        return carry

    lax.fori_loop(0, nodes // WIDTH, select_step, 0)

    for c in range(n_chunk):
        own[c].wait()
        for d in range(1, n_harm):
            arrive(d, c).wait_recv()
            start_halo(d, c)
    for load in loads:
        load.wait()

    def block_of(c, index):
        return jnp.concatenate([ext[c][h, index] for h in range(n_harm)], axis=0)

    half = chunk_rows // 2

    def local_step(i, carry):
        at = pl.ds(pl.multiple_of(i * WIDTH, WIDTH), WIDTH)
        first = row_blocks + i * (WIDTH // 128)
        pieces = [
            jnp.concatenate([block_of(c, first + t) for t in range(WIDTH // 128)], axis=1)
            for c in range(n_chunk)
        ]
        field = jnp.concatenate(pieces, axis=0) if n_chunk > 1 else pieces[0]
        samples = jnp.dot(fourier[...], field, preferred_element_type=jnp.float32)
        weighted = (rad[:, at].astype(jnp.float32) * samples).astype(jnp.bfloat16)
        radiative = jnp.dot(fourier_t[...], weighted, preferred_element_type=jnp.float32)
        cap = capacity[:, at]
        for c in range(n_chunk):
            lam = pieces[c].astype(jnp.float32)
            swapped = jnp.concatenate([lam[half:], lam[:half]], axis=0)
            rows = slice(c * chunk_rows, (c + 1) * chunk_rows)
            rate = rate_k[rows, :] * swapped
            rest = src[:, c, :, at].reshape(chunk_rows, WIDTH) - (cap * rate + radiative[rows])
            src[:, c, :, at] = rest.reshape(n_harm, ROWS, WIDTH)
        return carry

    lax.fori_loop(0, nodes // WIDTH, local_step, 0)

    group = nodes // GROUPS
    group_blocks = group // 128

    def back(d, c, q):
        peer = lax.rem(me_h + d, n_harm)
        return pltpu.make_async_remote_copy(
            src_ref=upd.at[peer, c, :, pl.ds(q * group, group)],
            dst_ref=ret.at[me_h, c, :, pl.ds(q * group, group)],
            send_sem=out_send.at[d, c, q],
            recv_sem=out_recv.at[d, c, q],
            device_id=(peer, me_n),
            device_id_type=MESH,
        )

    def own_back(c, q):
        return pltpu.make_async_copy(
            upd.at[me_h, c, :, pl.ds(q * group, group)],
            ret.at[me_h, c, :, pl.ds(q * group, group)],
            own_sem.at[c, q],
        )

    for c in range(n_chunk):
        for side in range(2):

            @pl.when(sides[1 - side][0])
            def _(side=side, c=c):
                for d in range(n_harm):
                    halo(d, c, side).wait_recv()

        for q in range(GROUPS):

            def block_step(i, carry, c=c, q=q):
                b = q * group_blocks + i
                at = pl.ds(pl.multiple_of(b * 128, 128), 128)
                lam = block_of(c, row_blocks + b)
                taken = [lam]
                for s in range(1, blk.shape[1]):
                    col = cols[s, b] - (pos - 1) * row_blocks
                    col = jnp.minimum(jnp.maximum(col, 0), 3 * row_blocks - 1)
                    taken.append(block_of(c, col))
                conductance = jnp.concatenate(
                    [blk[b, s] for s in range(blk.shape[1])], axis=1
                )
                conduction = lax.dot_general(
                    jnp.concatenate(taken, axis=1),
                    conductance,
                    NT,
                    preferred_element_type=jnp.float32,
                )
                residual = src[:, c, :, at].reshape(chunk_rows, 128) - conduction
                new = lam.astype(jnp.float32) + inv_diag[:, at] * residual
                upd[:, c, :, at] = new.astype(jnp.bfloat16).reshape(n_harm, ROWS, 128)
                return carry

            lax.fori_loop(0, group_blocks, block_step, 0, unroll=2)
            for d in range(1, n_harm):
                back(d, c, q).start()
            own_back(c, q).start()

    part[...] = jnp.zeros_like(part)

    def gradient_step(i, carry):
        at = pl.ds(pl.multiple_of(i * 512, 512), 512)
        new = upd[:, :, :, at].reshape(n_chunk * chunk_rows, 512)
        both = lax.dot_general(select[:, at], new, NT, preferred_element_type=jnp.float32)
        part[...] += both[0:128] + both[128:256]
        return carry

    lax.fori_loop(0, nodes // 512, gradient_step, 0)

    def hand_over(side):
        _, device, place = sides[side]
        rows = pl.ds(0 if side == 0 else 2 * ZONE_DEV, ZONE_DEV)
        return pltpu.make_async_remote_copy(
            src_ref=part.at[rows, :],
            dst_ref=from_next if side == 0 else from_prev,
            send_sem=part_send.at[side],
            recv_sem=part_recv.at[side],
            device_id=device,
            device_id_type=MESH,
        )

    for side in range(2):

        @pl.when(sides[side][0])
        def _(side=side):
            hand_over(side).start()

    grad[...] = part[ZONE_DEV : 2 * ZONE_DEV, :]

    for side, buffer in ((0, from_next), (1, from_prev)):

        @pl.when(sides[1 - side][0])
        def _(side=side, buffer=buffer):
            hand_over(side).wait_recv()
            grad[...] += buffer[...]

    for c in range(n_chunk):
        for q in range(GROUPS):
            own_back(c, q).wait()
            for d in range(1, n_harm):
                back(d, c, q).wait()
        for d in range(1, n_harm):
            arrive(d, c).wait_send()
    for side in range(2):

        @pl.when(sides[side][0])
        def _(side=side):
            hand_over(side).wait_send()
            for c in range(n_chunk):
                for d in range(n_harm):
                    halo(d, c, side).wait_send()


def body(
    n_harm,
    n_node,
    adjoint,
    source,
    rad_coeff,
    capacity,
    inv_diag,
    blocks,
    block_cols,
    zone_of,
    heater_weight,
):
    rows, _, nodes = adjoint.shape
    n_chunk = rows // ROWS
    harmonics = n_harm * rows
    order = np.arange(harmonics).reshape(n_harm, n_chunk, ROWS).transpose(1, 0, 2).reshape(-1)
    basis = fourier_basis(harmonics)
    half = harmonics // 2
    rate_k = np.where(order < half, order, -(order - half)).astype(np.float32)[:, None]
    rate_k = np.broadcast_to(rate_k, (harmonics, WIDTH))

    row_blocks = nodes // 128
    sent = adjoint.reshape(n_chunk, ROWS, n_harm, row_blocks, 128).transpose(2, 0, 3, 1, 4)
    vmem = pl.BlockSpec(memory_space=pltpu.VMEM)
    smem = pl.BlockSpec(memory_space=pltpu.SMEM)
    hbm = pl.BlockSpec(memory_space=pl.ANY)
    piece = (n_harm, n_chunk, ROWS, nodes)
    dma = pltpu.SemaphoreType.DMA
    returned, gradient = pl.pallas_call(
        functools.partial(kernel, n_harm, n_node, n_chunk),
        out_shape=(
            jax.ShapeDtypeStruct(piece, jnp.bfloat16),
            jax.ShapeDtypeStruct((ZONE_DEV, harmonics), jnp.float32),
        ),
        in_specs=[vmem, hbm, hbm, hbm, vmem, vmem, vmem, vmem, smem, vmem, vmem, vmem],
        out_specs=(vmem, vmem),
        scratch_shapes=[pltpu.VMEM((n_harm, 3 * row_blocks, ROWS, 128), jnp.bfloat16)] * n_chunk
        + [
            pltpu.VMEM(piece, jnp.float32),
            pltpu.VMEM(rad_coeff.shape, jnp.bfloat16),
            pltpu.VMEM(blocks.shape, jnp.bfloat16),
            pltpu.VMEM(piece, jnp.bfloat16),
            pltpu.VMEM((256, nodes), jnp.bfloat16),
            pltpu.VMEM((128, harmonics), jnp.float32),
            pltpu.VMEM((ZONE_DEV, harmonics), jnp.float32),
            pltpu.VMEM((ZONE_DEV, harmonics), jnp.float32),
            dma((3 + n_chunk,)),
            dma((n_harm, n_chunk)),
            dma((n_harm, n_chunk)),
            dma((2, n_harm, n_chunk)),
            dma((2, n_harm, n_chunk)),
            dma((n_harm, n_chunk, GROUPS)),
            dma((n_harm, n_chunk, GROUPS)),
            dma((n_chunk, GROUPS)),
            dma((2,)),
            dma((2,)),
        ],
        compiler_params=pltpu.CompilerParams(
            collective_id=0, has_side_effects=True, vmem_limit_bytes=48 * 2**20
        ),
    )(
        sent,
        source.reshape(piece),
        rad_coeff,
        blocks,
        capacity[None, :],
        inv_diag[None, :],
        heater_weight[None, :],
        zone_of[None, :],
        block_cols.T,
        jnp.asarray(basis[:, order]),
        jnp.asarray(basis.T[order]),
        jnp.asarray(rate_k),
    )
    return returned.reshape(n_harm, rows, nodes).transpose(1, 0, 2), gradient


def solution(mesh):
    in_specs = (
        P("harm", None, "node"),
        P(None, ("harm", "node")),
        P(None, ("harm", "node")),
        P(("harm", "node")),
        P(("harm", "node")),
        P(("harm", "node"), None, None, None),
        P(("harm", "node"), None),
        P(("harm", "node")),
        P(("harm", "node")),
    )
    out_specs = (P("harm", None, "node"), P(("harm", "node"), None))
    step = functools.partial(body, mesh.shape["harm"], mesh.shape["node"])
    return jax.shard_map(step, mesh=mesh, in_specs=in_specs, out_specs=out_specs, check_vma=False)
```

```python
import functools
import math

import jax
import jax.numpy as jnp
import numpy as np
from jax import lax
from jax.experimental import pallas as pl
from jax.experimental.pallas import tpu as pltpu
from jax.sharding import PartitionSpec as P

ZONE_DEV = 40
ROWS = 16
UNROLL = 4
GROUPS = 4
WIDTH = 512
MESH = pl.DeviceIdType.MESH
NT = (((1,), (1,)), ((), ()))


def fourier_basis(count):
    sample_index = np.arange(count, dtype=np.float32)[:, None]
    column_index = np.arange(count)[None, :]
    half_count = count // 2
    frequency = np.where(
        column_index <= half_count, column_index, column_index - half_count
    ).astype(np.float32)
    angle = np.float32(2.0 * math.pi) * frequency * sample_index / np.float32(count)
    values_table = np.where(column_index <= half_count, np.cos(angle), np.sin(angle))
    scaling = np.where(
        (column_index == 0) | (column_index == half_count),
        math.sqrt(1.0 / count),
        math.sqrt(2.0 / count),
    ).astype(np.float32)
    return (values_table * scaling).astype(jnp.bfloat16)


def kernel(
    n_harm,
    n_node,
    n_chunk,
    given,
    src_any,
    rad_any,
    blk_any,
    capacity,
    inv_diag,
    weight,
    zone,
    cols,
    fourier,
    fourier_t,
    rate_k,
    ret,
    grad,
    *scratch,
):
    ext = scratch[:n_chunk]
    (
        adj,
        src,
        rad,
        blk,
        upd,
        select,
        part,
        from_prev,
        from_next,
        load_sem,
        in_send,
        in_recv,
        halo_send,
        halo_recv,
        out_send,
        out_recv,
        own_sem,
        part_send,
        part_recv,
    ) = scratch[n_chunk:]
    nodes = given.shape[2]
    row_blocks = nodes // 128
    chunk_rows = n_harm * ROWS
    me_h = lax.axis_index("harm")
    me_n = lax.axis_index("node")
    pos = me_h * n_node + me_n
    last = n_harm * n_node - 1
    has_prev = pos > 0
    has_next = pos < last
    prev = jnp.maximum(pos - 1, 0)
    following = jnp.minimum(pos + 1, last)
    prev_id = (prev // n_node, prev % n_node)
    next_id = (following // n_node, following % n_node)
    sides = ((has_prev, prev_id, 2), (has_next, next_id, 0))

    loads = [
        pltpu.make_async_copy(src_any, src, load_sem.at[0]),
        pltpu.make_async_copy(rad_any, rad, load_sem.at[1]),
        pltpu.make_async_copy(blk_any, blk, load_sem.at[2]),
    ]
    own = [
        pltpu.make_async_copy(
            adj.at[me_h, c], ext[c].at[me_h, pl.ds(row_blocks, row_blocks)], load_sem.at[3 + c]
        )
        for c in range(n_chunk)
    ]

    barrier = pltpu.get_barrier_semaphore()
    for d in range(1, n_harm):
        peer = lax.rem(me_h + d, n_harm)
        pl.semaphore_signal(barrier, inc=1, device_id=(peer, me_n), device_id_type=MESH)
    for there, device, _ in sides:

        @pl.when(there)
        def _(device=device):
            pl.semaphore_signal(barrier, inc=1, device_id=device, device_id_type=MESH)

    pl.semaphore_wait(
        barrier, n_harm - 1 + has_prev.astype(jnp.int32) + has_next.astype(jnp.int32)
    )

    def arrive(d, c):
        peer = lax.rem(me_h + d, n_harm)
        return pltpu.make_async_remote_copy(
            src_ref=adj.at[peer, c],
            dst_ref=ext[c].at[me_h, pl.ds(row_blocks, row_blocks)],
            send_sem=in_send.at[d, c],
            recv_sem=in_recv.at[d, c],
            device_id=(peer, me_n),
            device_id_type=MESH,
        )

    def halo(d, c, side):
        _, device, place = sides[side]
        piece = lax.rem(me_h - d + n_harm, n_harm)
        if d == 0:
            source = adj.at[me_h, c]
        else:
            source = ext[c].at[piece, pl.ds(row_blocks, row_blocks)]
        return pltpu.make_async_remote_copy(
            src_ref=source,
            dst_ref=ext[c].at[piece, pl.ds(place * row_blocks, row_blocks)],
            send_sem=halo_send.at[side, d, c],
            recv_sem=halo_recv.at[side, d, c],
            device_id=device,
            device_id_type=MESH,
        )

    def start_halo(d, c):
        for side in range(2):

            @pl.when(sides[side][0])
            def _(side=side):
                halo(d, c, side).start()

    def split(h, c):
        for i in range(row_blocks):
            adj[h, c, i] = given[h, c * ROWS : (c + 1) * ROWS, i * 128 : (i + 1) * 128]

    for c in range(n_chunk):
        for d in range(1, n_harm):
            split(lax.rem(me_h + d, n_harm), c)
            arrive(d, c).start()
        split(me_h, c)
        own[c].start()
        start_halo(0, c)
        if c == 0:
            for load in loads:
                load.start()

    zone_row = lax.broadcasted_iota(jnp.int32, (128, WIDTH), 0)

    def select_step(i, carry):
        at = pl.ds(pl.multiple_of(i * WIDTH, WIDTH), WIDTH)
        hit = zone_row == (zone[:, at] - (pos - 1) * ZONE_DEV)
        w = weight[:, at]
        high = w.astype(jnp.bfloat16).astype(jnp.float32)
        select[0:128, at] = jnp.where(hit, high, 0.0).astype(jnp.bfloat16)
        select[128:256, at] = jnp.where(hit, w - high, 0.0).astype(jnp.bfloat16)
        return carry

    lax.fori_loop(0, nodes // WIDTH, select_step, 0)

    def block_of(c, index):
        return jnp.concatenate([ext[c][h, index] for h in range(n_harm)], axis=0)

    group = nodes // GROUPS
    half = chunk_rows // 2

    def back(d, c, q):
        peer = lax.rem(me_h + d, n_harm)
        return pltpu.make_async_remote_copy(
            src_ref=upd.at[peer, c, :, pl.ds(q * group, group)],
            dst_ref=ret.at[me_h, c, :, pl.ds(q * group, group)],
            send_sem=out_send.at[d, c, q],
            recv_sem=out_recv.at[d, c, q],
            device_id=(peer, me_n),
            device_id_type=MESH,
        )

    def own_back(c, q):
        return pltpu.make_async_copy(
            upd.at[me_h, c, :, pl.ds(q * group, group)],
            ret.at[me_h, c, :, pl.ds(q * group, group)],
            own_sem.at[c, q],
        )

    def start_back(c, q):
        for d in range(1, n_harm):
            back(d, c, q).start()
        own_back(c, q).start()

    def wait_halo(c):
        for side in range(2):

            @pl.when(sides[1 - side][0])
            def _(side=side):
                for d in range(n_harm):
                    halo(d, c, side).wait_recv()

    def conduct(c, start, finish):
        results = []
        for u in range(UNROLL):
            b = start + u
            at = pl.ds(pl.multiple_of(b * 128, 128), 128)
            lam = block_of(c, row_blocks + b)
            taken = [lam]
            for s in range(1, blk.shape[1]):
                col = cols[s, b] - (pos - 1) * row_blocks
                col = jnp.minimum(jnp.maximum(col, 0), 3 * row_blocks - 1)
                taken.append(block_of(c, col))
            conduction = lax.dot_general(
                jnp.concatenate(taken, axis=1),
                jnp.concatenate([blk[b, s] for s in range(blk.shape[1])], axis=1),
                NT,
                preferred_element_type=jnp.float32,
            )
            residual = src[:, c, :, at].reshape(chunk_rows, 128) - conduction
            if finish:
                residual = lam.astype(jnp.float32) + inv_diag[:, at] * residual
            results.append((at, residual))
        for at, result in results:
            result = result.reshape(n_harm, ROWS, 128)
            if finish:
                upd[:, c, :, at] = result.astype(jnp.bfloat16)
            else:
                src[:, c, :, at] = result

    last_chunk = n_chunk - 1
    for c in range(n_chunk):
        own[c].wait()
        for d in range(1, n_harm):
            arrive(d, c).wait_recv()
            start_halo(d, c)
        if c == 0:
            for load in loads:
                load.wait()
        if c < last_chunk:
            wait_halo(c)

            def conduct_step(i, carry, c=c):
                conduct(c, i * UNROLL, False)
                return carry

            lax.fori_loop(0, row_blocks // UNROLL, conduct_step, 0)

    def local_step(i, carry):
        at = pl.ds(pl.multiple_of(i * WIDTH, WIDTH), WIDTH)
        first = row_blocks + i * (WIDTH // 128)
        pieces = [
            jnp.concatenate([block_of(c, first + t) for t in range(WIDTH // 128)], axis=1)
            for c in range(n_chunk)
        ]
        field = jnp.concatenate(pieces, axis=0) if n_chunk > 1 else pieces[0]
        samples = jnp.dot(fourier[...], field, preferred_element_type=jnp.float32)
        weighted = (rad[:, at].astype(jnp.float32) * samples).astype(jnp.bfloat16)
        radiative = jnp.dot(fourier_t[...], weighted, preferred_element_type=jnp.float32)
        cap = capacity[:, at]
        for c in range(n_chunk):
            lam = pieces[c].astype(jnp.float32)
            swapped = jnp.concatenate([lam[half:], lam[:half]], axis=0)
            rows = slice(c * chunk_rows, (c + 1) * chunk_rows)
            rate = rate_k[rows, :] * swapped
            rest = src[:, c, :, at].reshape(chunk_rows, WIDTH) - (cap * rate + radiative[rows])
            if c < last_chunk:
                new = lam + inv_diag[:, at] * rest
                upd[:, c, :, at] = new.astype(jnp.bfloat16).reshape(n_harm, ROWS, WIDTH)
            else:
                src[:, c, :, at] = rest.reshape(n_harm, ROWS, WIDTH)
        return carry

    steps = group // WIDTH
    for q in range(GROUPS):
        lax.fori_loop(q * steps, (q + 1) * steps, local_step, 0)
        for c in range(last_chunk):
            start_back(c, q)

    wait_halo(last_chunk)
    group_steps = group // 128 // UNROLL
    for q in range(GROUPS):

        def final_step(i, carry):
            conduct(last_chunk, i * UNROLL, True)
            return carry

        lax.fori_loop(q * group_steps, (q + 1) * group_steps, final_step, 0)
        start_back(last_chunk, q)

    part[...] = jnp.zeros_like(part)

    def gradient_step(i, carry):
        at = pl.ds(pl.multiple_of(i * 512, 512), 512)
        new = upd[:, :, :, at].reshape(n_chunk * chunk_rows, 512)
        both = lax.dot_general(select[:, at], new, NT, preferred_element_type=jnp.float32)
        part[...] += both[0:128] + both[128:256]
        return carry

    lax.fori_loop(0, nodes // 512, gradient_step, 0)

    def hand_over(side):
        _, device, place = sides[side]
        rows = pl.ds(0 if side == 0 else 2 * ZONE_DEV, ZONE_DEV)
        return pltpu.make_async_remote_copy(
            src_ref=part.at[rows, :],
            dst_ref=from_next if side == 0 else from_prev,
            send_sem=part_send.at[side],
            recv_sem=part_recv.at[side],
            device_id=device,
            device_id_type=MESH,
        )

    for side in range(2):

        @pl.when(sides[side][0])
        def _(side=side):
            hand_over(side).start()

    grad[...] = part[ZONE_DEV : 2 * ZONE_DEV, :]

    for side, buffer in ((0, from_next), (1, from_prev)):

        @pl.when(sides[1 - side][0])
        def _(side=side, buffer=buffer):
            hand_over(side).wait_recv()
            grad[...] += buffer[...]

    for c in range(n_chunk):
        for q in range(GROUPS):
            own_back(c, q).wait()
            for d in range(1, n_harm):
                back(d, c, q).wait()
        for d in range(1, n_harm):
            arrive(d, c).wait_send()
    for side in range(2):

        @pl.when(sides[side][0])
        def _(side=side):
            hand_over(side).wait_send()
            for c in range(n_chunk):
                for d in range(n_harm):
                    halo(d, c, side).wait_send()


def body(
    n_harm,
    n_node,
    adjoint,
    source,
    rad_coeff,
    capacity,
    inv_diag,
    blocks,
    block_cols,
    zone_of,
    heater_weight,
):
    rows, _, nodes = adjoint.shape
    n_chunk = rows // ROWS
    harmonics = n_harm * rows
    order = np.arange(harmonics).reshape(n_harm, n_chunk, ROWS).transpose(1, 0, 2).reshape(-1)
    basis = fourier_basis(harmonics)
    half = harmonics // 2
    rate_k = np.where(order < half, order, -(order - half)).astype(np.float32)[:, None]
    rate_k = np.broadcast_to(rate_k, (harmonics, WIDTH))

    row_blocks = nodes // 128
    sent = adjoint.transpose(1, 0, 2)
    vmem = pl.BlockSpec(memory_space=pltpu.VMEM)
    smem = pl.BlockSpec(memory_space=pltpu.SMEM)
    hbm = pl.BlockSpec(memory_space=pl.ANY)
    piece = (n_harm, n_chunk, ROWS, nodes)
    dma = pltpu.SemaphoreType.DMA
    returned, gradient = pl.pallas_call(
        functools.partial(kernel, n_harm, n_node, n_chunk),
        out_shape=(
            jax.ShapeDtypeStruct(piece, jnp.bfloat16),
            jax.ShapeDtypeStruct((ZONE_DEV, harmonics), jnp.float32),
        ),
        in_specs=[vmem, hbm, hbm, hbm, vmem, vmem, vmem, vmem, smem, vmem, vmem, vmem],
        out_specs=(vmem, vmem),
        scratch_shapes=[pltpu.VMEM((n_harm, 3 * row_blocks, ROWS, 128), jnp.bfloat16)] * n_chunk
        + [
            pltpu.VMEM((n_harm, n_chunk, row_blocks, ROWS, 128), jnp.bfloat16),
            pltpu.VMEM(piece, jnp.float32),
            pltpu.VMEM(rad_coeff.shape, jnp.bfloat16),
            pltpu.VMEM(blocks.shape, jnp.bfloat16),
            pltpu.VMEM(piece, jnp.bfloat16),
            pltpu.VMEM((256, nodes), jnp.bfloat16),
            pltpu.VMEM((128, harmonics), jnp.float32),
            pltpu.VMEM((ZONE_DEV, harmonics), jnp.float32),
            pltpu.VMEM((ZONE_DEV, harmonics), jnp.float32),
            dma((3 + n_chunk,)),
            dma((n_harm, n_chunk)),
            dma((n_harm, n_chunk)),
            dma((2, n_harm, n_chunk)),
            dma((2, n_harm, n_chunk)),
            dma((n_harm, n_chunk, GROUPS)),
            dma((n_harm, n_chunk, GROUPS)),
            dma((n_chunk, GROUPS)),
            dma((2,)),
            dma((2,)),
        ],
        compiler_params=pltpu.CompilerParams(
            collective_id=0, has_side_effects=True, vmem_limit_bytes=48 * 2**20
        ),
    )(
        sent,
        source.reshape(piece),
        rad_coeff,
        blocks,
        capacity[None, :],
        inv_diag[None, :],
        heater_weight[None, :],
        zone_of[None, :],
        block_cols.T,
        jnp.asarray(basis[:, order]),
        jnp.asarray(basis.T[order]),
        jnp.asarray(rate_k),
    )
    return returned.reshape(n_harm, rows, nodes).transpose(1, 0, 2), gradient


def solution(mesh):
    in_specs = (
        P("harm", None, "node"),
        P(None, ("harm", "node")),
        P(None, ("harm", "node")),
        P(("harm", "node")),
        P(("harm", "node")),
        P(("harm", "node"), None, None, None),
        P(("harm", "node"), None),
        P(("harm", "node")),
        P(("harm", "node")),
    )
    out_specs = (P("harm", None, "node"), P(("harm", "node"), None))
    step = functools.partial(body, mesh.shape["harm"], mesh.shape["node"])
    return jax.shard_map(step, mesh=mesh, in_specs=in_specs, out_specs=out_specs, check_vma=False)
```

```python
import functools
import math

import jax
import jax.numpy as jnp
import numpy as np
from jax import lax
from jax.experimental import pallas as pl
from jax.experimental.pallas import tpu as pltpu
from jax.sharding import PartitionSpec as P

ZONE_DEV = 40
ROWS = 16
UNROLL = 4
GROUPS = 4
WIDTH = 512
MESH = pl.DeviceIdType.MESH
NT = (((1,), (1,)), ((), ()))


def fourier_basis(count):
    sample_index = np.arange(count, dtype=np.float32)[:, None]
    column_index = np.arange(count)[None, :]
    half_count = count // 2
    frequency = np.where(
        column_index <= half_count, column_index, column_index - half_count
    ).astype(np.float32)
    angle = np.float32(2.0 * math.pi) * frequency * sample_index / np.float32(count)
    values_table = np.where(column_index <= half_count, np.cos(angle), np.sin(angle))
    scaling = np.where(
        (column_index == 0) | (column_index == half_count),
        math.sqrt(1.0 / count),
        math.sqrt(2.0 / count),
    ).astype(np.float32)
    return (values_table * scaling).astype(jnp.bfloat16)


def kernel(
    n_harm,
    n_node,
    n_chunk,
    given,
    src_any,
    rad_any,
    blk_any,
    cap_any,
    inv_any,
    weight_any,
    zone_any,
    cols,
    fourier_any,
    fourier_t_any,
    ret,
    grad,
    *scratch,
):
    ext = scratch[:n_chunk]
    (
        capacity,
        inv_diag,
        weight,
        zone,
        fourier,
        fourier_t,
        adj,
        src,
        rad,
        blk,
        upd,
        select,
        part,
        from_prev,
        from_next,
        load_sem,
        in_send,
        in_recv,
        halo_send,
        halo_recv,
        out_send,
        out_recv,
        own_sem,
        part_send,
        part_recv,
        small_sem,
    ) = scratch[n_chunk:]
    nodes = given.shape[2]
    row_blocks = nodes // 128
    chunk_rows = n_harm * ROWS
    me_h = lax.axis_index("harm")
    me_n = lax.axis_index("node")
    pos = me_h * n_node + me_n
    last = n_harm * n_node - 1
    has_prev = pos > 0
    has_next = pos < last
    prev = jnp.maximum(pos - 1, 0)
    following = jnp.minimum(pos + 1, last)
    prev_id = (prev // n_node, prev % n_node)
    next_id = (following // n_node, following % n_node)
    sides = ((has_prev, prev_id, 2), (has_next, next_id, 0))

    loads = [
        pltpu.make_async_copy(src_any, src, load_sem.at[0]),
        pltpu.make_async_copy(rad_any, rad, load_sem.at[1]),
        pltpu.make_async_copy(blk_any, blk, load_sem.at[2]),
    ]
    own = [
        pltpu.make_async_copy(
            adj.at[me_h, c], ext[c].at[me_h, pl.ds(row_blocks, row_blocks)], load_sem.at[3 + c]
        )
        for c in range(n_chunk)
    ]

    small = [
        pltpu.make_async_copy(source, target, small_sem.at[i])
        for i, (source, target) in enumerate(
            (
                (zone_any, zone),
                (weight_any, weight),
                (cap_any, capacity),
                (inv_any, inv_diag),
                (fourier_any, fourier),
                (fourier_t_any, fourier_t),
            )
        )
    ]
    for load in small:
        load.start()

    barrier = pltpu.get_barrier_semaphore()
    for d in range(1, n_harm):
        peer = lax.rem(me_h + d, n_harm)
        pl.semaphore_signal(barrier, inc=1, device_id=(peer, me_n), device_id_type=MESH)
    for there, device, _ in sides:

        @pl.when(there)
        def _(device=device):
            pl.semaphore_signal(barrier, inc=1, device_id=device, device_id_type=MESH)

    pl.semaphore_wait(
        barrier, n_harm - 1 + has_prev.astype(jnp.int32) + has_next.astype(jnp.int32)
    )

    def arrive(d, c):
        peer = lax.rem(me_h + d, n_harm)
        return pltpu.make_async_remote_copy(
            src_ref=adj.at[peer, c],
            dst_ref=ext[c].at[me_h, pl.ds(row_blocks, row_blocks)],
            send_sem=in_send.at[d, c],
            recv_sem=in_recv.at[d, c],
            device_id=(peer, me_n),
            device_id_type=MESH,
        )

    def halo(d, c, side):
        _, device, place = sides[side]
        piece = lax.rem(me_h - d + n_harm, n_harm)
        if d == 0:
            source = adj.at[me_h, c]
        else:
            source = ext[c].at[piece, pl.ds(row_blocks, row_blocks)]
        return pltpu.make_async_remote_copy(
            src_ref=source,
            dst_ref=ext[c].at[piece, pl.ds(place * row_blocks, row_blocks)],
            send_sem=halo_send.at[side, d, c],
            recv_sem=halo_recv.at[side, d, c],
            device_id=device,
            device_id_type=MESH,
        )

    def start_halo(d, c):
        for side in range(2):

            @pl.when(sides[side][0])
            def _(side=side):
                halo(d, c, side).start()

    def split(h, c):
        for i in range(row_blocks):
            adj[h, c, i] = given[h, c * ROWS : (c + 1) * ROWS, i * 128 : (i + 1) * 128]

    for c in range(n_chunk):
        for d in range(1, n_harm):
            split(lax.rem(me_h + d, n_harm), c)
            arrive(d, c).start()
        split(me_h, c)
        own[c].start()
        start_halo(0, c)
        if c == 0:
            for load in loads:
                load.start()

    for load in small:
        load.wait()

    zone_row = lax.broadcasted_iota(jnp.int32, (128, WIDTH), 0)

    def select_step(i, carry):
        at = pl.ds(pl.multiple_of(i * WIDTH, WIDTH), WIDTH)
        hit = zone_row == (zone[:, at] - (pos - 1) * ZONE_DEV)
        w = weight[:, at]
        high = w.astype(jnp.bfloat16).astype(jnp.float32)
        select[0:128, at] = jnp.where(hit, high, 0.0).astype(jnp.bfloat16)
        select[128:256, at] = jnp.where(hit, w - high, 0.0).astype(jnp.bfloat16)
        return carry

    lax.fori_loop(0, nodes // WIDTH, select_step, 0)

    def block_of(c, index):
        return jnp.concatenate([ext[c][h, index] for h in range(n_harm)], axis=0)

    group = nodes // GROUPS
    half = chunk_rows // 2

    def back(d, c, q):
        peer = lax.rem(me_h + d, n_harm)
        return pltpu.make_async_remote_copy(
            src_ref=upd.at[peer, c, :, pl.ds(q * group, group)],
            dst_ref=ret.at[me_h, c, :, pl.ds(q * group, group)],
            send_sem=out_send.at[d, c, q],
            recv_sem=out_recv.at[d, c, q],
            device_id=(peer, me_n),
            device_id_type=MESH,
        )

    def own_back(c, q):
        return pltpu.make_async_copy(
            upd.at[me_h, c, :, pl.ds(q * group, group)],
            ret.at[me_h, c, :, pl.ds(q * group, group)],
            own_sem.at[c, q],
        )

    def start_back(c, q):
        for d in range(1, n_harm):
            back(d, c, q).start()
        own_back(c, q).start()

    def wait_halo(c):
        for side in range(2):

            @pl.when(sides[1 - side][0])
            def _(side=side):
                for d in range(n_harm):
                    halo(d, c, side).wait_recv()

    def conduct(c, start, finish):
        results = []
        for u in range(UNROLL):
            b = start + u
            at = pl.ds(pl.multiple_of(b * 128, 128), 128)
            lam = block_of(c, row_blocks + b)
            taken = [lam]
            for s in range(1, blk.shape[1]):
                col = cols[s, b] - (pos - 1) * row_blocks
                col = jnp.minimum(jnp.maximum(col, 0), 3 * row_blocks - 1)
                taken.append(block_of(c, col))
            conduction = lax.dot_general(
                jnp.concatenate(taken, axis=1),
                jnp.concatenate([blk[b, s] for s in range(blk.shape[1])], axis=1),
                NT,
                preferred_element_type=jnp.float32,
            )
            residual = src[:, c, :, at].reshape(chunk_rows, 128) - conduction
            if finish:
                residual = lam.astype(jnp.float32) + inv_diag[:, at] * residual
            results.append((at, residual))
        for at, result in results:
            result = result.reshape(n_harm, ROWS, 128)
            if finish:
                upd[:, c, :, at] = result.astype(jnp.bfloat16)
            else:
                src[:, c, :, at] = result

    last_chunk = n_chunk - 1
    for c in range(n_chunk):
        own[c].wait()
        for d in range(1, n_harm):
            arrive(d, c).wait_recv()
            start_halo(d, c)
        if c == 0:
            for load in loads:
                load.wait()
        if c < last_chunk:
            wait_halo(c)

            def conduct_step(i, carry, c=c):
                conduct(c, i * UNROLL, False)
                return carry

            lax.fori_loop(0, row_blocks // UNROLL, conduct_step, 0)

    row = lax.broadcasted_iota(jnp.int32, (chunk_rows, WIDTH), 0)
    rate_k = []
    for c in range(n_chunk):
        natural = (row // ROWS) * (n_chunk * ROWS) + c * ROWS + row % ROWS
        middle = n_chunk * n_harm * ROWS // 2
        rate_k.append(jnp.where(natural < middle, natural, middle - natural).astype(jnp.float32))

    def local_step(i, carry):
        at = pl.ds(pl.multiple_of(i * WIDTH, WIDTH), WIDTH)
        first = row_blocks + i * (WIDTH // 128)
        pieces = [
            jnp.concatenate([block_of(c, first + t) for t in range(WIDTH // 128)], axis=1)
            for c in range(n_chunk)
        ]
        field = jnp.concatenate(pieces, axis=0) if n_chunk > 1 else pieces[0]
        samples = jnp.dot(fourier[...], field, preferred_element_type=jnp.float32)
        weighted = (rad[:, at].astype(jnp.float32) * samples).astype(jnp.bfloat16)
        radiative = jnp.dot(fourier_t[...], weighted, preferred_element_type=jnp.float32)
        cap = capacity[:, at]
        for c in range(n_chunk):
            lam = pieces[c].astype(jnp.float32)
            swapped = jnp.concatenate([lam[half:], lam[:half]], axis=0)
            rows = slice(c * chunk_rows, (c + 1) * chunk_rows)
            rate = rate_k[c] * swapped
            rest = src[:, c, :, at].reshape(chunk_rows, WIDTH) - (cap * rate + radiative[rows])
            if c < last_chunk:
                new = lam + inv_diag[:, at] * rest
                upd[:, c, :, at] = new.astype(jnp.bfloat16).reshape(n_harm, ROWS, WIDTH)
            else:
                src[:, c, :, at] = rest.reshape(n_harm, ROWS, WIDTH)
        return carry

    steps = group // WIDTH
    for q in range(GROUPS):
        lax.fori_loop(q * steps, (q + 1) * steps, local_step, 0)
        for c in range(last_chunk):
            start_back(c, q)

    wait_halo(last_chunk)
    group_steps = group // 128 // UNROLL
    for q in range(GROUPS):

        def final_step(i, carry):
            conduct(last_chunk, i * UNROLL, True)
            return carry

        lax.fori_loop(q * group_steps, (q + 1) * group_steps, final_step, 0)
        start_back(last_chunk, q)

    part[...] = jnp.zeros_like(part)

    def gradient_step(i, carry):
        at = pl.ds(pl.multiple_of(i * 512, 512), 512)
        new = upd[:, :, :, at].reshape(n_chunk * chunk_rows, 512)
        both = lax.dot_general(select[:, at], new, NT, preferred_element_type=jnp.float32)
        part[...] += both[0:128] + both[128:256]
        return carry

    lax.fori_loop(0, nodes // 512, gradient_step, 0)

    def hand_over(side):
        _, device, place = sides[side]
        rows = pl.ds(0 if side == 0 else 2 * ZONE_DEV, ZONE_DEV)
        return pltpu.make_async_remote_copy(
            src_ref=part.at[rows, :],
            dst_ref=from_next if side == 0 else from_prev,
            send_sem=part_send.at[side],
            recv_sem=part_recv.at[side],
            device_id=device,
            device_id_type=MESH,
        )

    for side in range(2):

        @pl.when(sides[side][0])
        def _(side=side):
            hand_over(side).start()

    grad[...] = part[ZONE_DEV : 2 * ZONE_DEV, :]

    for side, buffer in ((0, from_next), (1, from_prev)):

        @pl.when(sides[1 - side][0])
        def _(side=side, buffer=buffer):
            hand_over(side).wait_recv()
            grad[...] += buffer[...]

    for c in range(n_chunk):
        for q in range(GROUPS):
            own_back(c, q).wait()
            for d in range(1, n_harm):
                back(d, c, q).wait()
        for d in range(1, n_harm):
            arrive(d, c).wait_send()
    for side in range(2):

        @pl.when(sides[side][0])
        def _(side=side):
            hand_over(side).wait_send()
            for c in range(n_chunk):
                for d in range(n_harm):
                    halo(d, c, side).wait_send()


def body(
    n_harm,
    n_node,
    adjoint,
    source,
    rad_coeff,
    capacity,
    inv_diag,
    blocks,
    block_cols,
    zone_of,
    heater_weight,
):
    rows, _, nodes = adjoint.shape
    n_chunk = rows // ROWS
    harmonics = n_harm * rows
    order = np.arange(harmonics).reshape(n_harm, n_chunk, ROWS).transpose(1, 0, 2).reshape(-1)
    basis = fourier_basis(harmonics)

    row_blocks = nodes // 128
    sent = adjoint.transpose(1, 0, 2)
    vmem = pl.BlockSpec(memory_space=pltpu.VMEM)
    smem = pl.BlockSpec(memory_space=pltpu.SMEM)
    hbm = pl.BlockSpec(memory_space=pl.ANY)
    piece = (n_harm, n_chunk, ROWS, nodes)
    dma = pltpu.SemaphoreType.DMA
    returned, gradient = pl.pallas_call(
        functools.partial(kernel, n_harm, n_node, n_chunk),
        out_shape=(
            jax.ShapeDtypeStruct(piece, jnp.bfloat16),
            jax.ShapeDtypeStruct((ZONE_DEV, harmonics), jnp.float32),
        ),
        in_specs=[vmem] + [hbm] * 7 + [smem, hbm, hbm],
        out_specs=(vmem, vmem),
        scratch_shapes=[pltpu.VMEM((n_harm, 3 * row_blocks, ROWS, 128), jnp.bfloat16)] * n_chunk
        + [
            pltpu.VMEM((1, nodes), jnp.float32),
            pltpu.VMEM((1, nodes), jnp.float32),
            pltpu.VMEM((1, nodes), jnp.float32),
            pltpu.VMEM((1, nodes), jnp.int32),
            pltpu.VMEM((harmonics, harmonics), jnp.bfloat16),
            pltpu.VMEM((harmonics, harmonics), jnp.bfloat16),
            pltpu.VMEM((n_harm, n_chunk, row_blocks, ROWS, 128), jnp.bfloat16),
            pltpu.VMEM(piece, jnp.float32),
            pltpu.VMEM(rad_coeff.shape, jnp.bfloat16),
            pltpu.VMEM(blocks.shape, jnp.bfloat16),
            pltpu.VMEM(piece, jnp.bfloat16),
            pltpu.VMEM((256, nodes), jnp.bfloat16),
            pltpu.VMEM((128, harmonics), jnp.float32),
            pltpu.VMEM((ZONE_DEV, harmonics), jnp.float32),
            pltpu.VMEM((ZONE_DEV, harmonics), jnp.float32),
            dma((3 + n_chunk,)),
            dma((n_harm, n_chunk)),
            dma((n_harm, n_chunk)),
            dma((2, n_harm, n_chunk)),
            dma((2, n_harm, n_chunk)),
            dma((n_harm, n_chunk, GROUPS)),
            dma((n_harm, n_chunk, GROUPS)),
            dma((n_chunk, GROUPS)),
            dma((2,)),
            dma((2,)),
            dma((6,)),
        ],
        compiler_params=pltpu.CompilerParams(
            collective_id=0, has_side_effects=True, vmem_limit_bytes=48 * 2**20
        ),
    )(
        sent,
        source.reshape(piece),
        rad_coeff,
        blocks,
        capacity[None, :],
        inv_diag[None, :],
        heater_weight[None, :],
        zone_of[None, :],
        block_cols.T,
        jnp.asarray(basis[:, order]),
        jnp.asarray(basis.T[order]),
    )
    return returned.reshape(n_harm, rows, nodes).transpose(1, 0, 2), gradient


def solution(mesh):
    in_specs = (
        P("harm", None, "node"),
        P(None, ("harm", "node")),
        P(None, ("harm", "node")),
        P(("harm", "node")),
        P(("harm", "node")),
        P(("harm", "node"), None, None, None),
        P(("harm", "node"), None),
        P(("harm", "node")),
        P(("harm", "node")),
    )
    out_specs = (P("harm", None, "node"), P(("harm", "node"), None))
    step = functools.partial(body, mesh.shape["harm"], mesh.shape["node"])
    return jax.shard_map(step, mesh=mesh, in_specs=in_specs, out_specs=out_specs, check_vma=False)
```

```python
import functools
import math

import jax
import jax.numpy as jnp
import numpy as np
from jax import lax
from jax.experimental import pallas as pl
from jax.experimental.pallas import tpu as pltpu
from jax.sharding import PartitionSpec as P

ZONE_DEV = 40
ROWS = 16
UNROLL = 4
GROUPS = 4
WIDTH = 512
MESH = pl.DeviceIdType.MESH
NT = (((1,), (1,)), ((), ()))


def fourier_basis(count):
    sample_index = np.arange(count, dtype=np.float32)[:, None]
    column_index = np.arange(count)[None, :]
    half_count = count // 2
    frequency = np.where(
        column_index <= half_count, column_index, column_index - half_count
    ).astype(np.float32)
    angle = np.float32(2.0 * math.pi) * frequency * sample_index / np.float32(count)
    values_table = np.where(column_index <= half_count, np.cos(angle), np.sin(angle))
    scaling = np.where(
        (column_index == 0) | (column_index == half_count),
        math.sqrt(1.0 / count),
        math.sqrt(2.0 / count),
    ).astype(np.float32)
    return (values_table * scaling).astype(jnp.bfloat16)


def kernel(
    n_harm,
    n_node,
    n_chunk,
    given,
    src_any,
    rad_any,
    blk_any,
    cap_any,
    inv_any,
    weight_any,
    zone_any,
    cols,
    fourier_any,
    fourier_t_any,
    ret,
    grad,
    *scratch,
):
    ext = scratch[:n_chunk]
    (
        capacity,
        inv_diag,
        weight,
        zone,
        fourier,
        fourier_t,
        adj,
        src,
        rad,
        blk,
        upd,
        select,
        part,
        from_prev,
        from_next,
        load_sem,
        in_send,
        in_recv,
        halo_send,
        halo_recv,
        out_send,
        out_recv,
        own_sem,
        part_send,
        part_recv,
        small_sem,
    ) = scratch[n_chunk:]
    nodes = given.shape[2]
    row_blocks = nodes // 128
    chunk_rows = n_harm * ROWS
    me_h = lax.axis_index("harm")
    me_n = lax.axis_index("node")
    pos = me_h * n_node + me_n
    last = n_harm * n_node - 1
    has_prev = pos > 0
    has_next = pos < last
    prev = jnp.maximum(pos - 1, 0)
    following = jnp.minimum(pos + 1, last)
    prev_id = (prev // n_node, prev % n_node)
    next_id = (following // n_node, following % n_node)
    sides = ((has_prev, prev_id, 2), (has_next, next_id, 0))

    loads = [
        pltpu.make_async_copy(src_any, src, load_sem.at[0]),
        pltpu.make_async_copy(rad_any, rad, load_sem.at[1]),
        pltpu.make_async_copy(blk_any, blk, load_sem.at[2]),
    ]
    own = [
        pltpu.make_async_copy(
            adj.at[me_h, c], ext[c].at[me_h, pl.ds(row_blocks, row_blocks)], load_sem.at[3 + c]
        )
        for c in range(n_chunk)
    ]

    small = [
        pltpu.make_async_copy(source, target, small_sem.at[i])
        for i, (source, target) in enumerate(
            (
                (zone_any, zone),
                (weight_any, weight),
                (cap_any, capacity),
                (inv_any, inv_diag),
                (fourier_any, fourier),
                (fourier_t_any, fourier_t),
            )
        )
    ]
    for load in small:
        load.start()

    barrier = pltpu.get_barrier_semaphore()
    for d in range(1, n_harm):
        peer = lax.rem(me_h + d, n_harm)
        pl.semaphore_signal(barrier, inc=1, device_id=(peer, me_n), device_id_type=MESH)
    for there, device, _ in sides:

        @pl.when(there)
        def _(device=device):
            pl.semaphore_signal(barrier, inc=1, device_id=device, device_id_type=MESH)

    pl.semaphore_wait(
        barrier, n_harm - 1 + has_prev.astype(jnp.int32) + has_next.astype(jnp.int32)
    )

    def arrive(d, c):
        peer = lax.rem(me_h + d, n_harm)
        return pltpu.make_async_remote_copy(
            src_ref=adj.at[peer, c],
            dst_ref=ext[c].at[me_h, pl.ds(row_blocks, row_blocks)],
            send_sem=in_send.at[d, c],
            recv_sem=in_recv.at[d, c],
            device_id=(peer, me_n),
            device_id_type=MESH,
        )

    def halo(d, c, side):
        _, device, place = sides[side]
        piece = lax.rem(me_h - d + n_harm, n_harm)
        if d == 0:
            source = adj.at[me_h, c]
        else:
            source = ext[c].at[piece, pl.ds(row_blocks, row_blocks)]
        return pltpu.make_async_remote_copy(
            src_ref=source,
            dst_ref=ext[c].at[piece, pl.ds(place * row_blocks, row_blocks)],
            send_sem=halo_send.at[side, d, c],
            recv_sem=halo_recv.at[side, d, c],
            device_id=device,
            device_id_type=MESH,
        )

    def start_halo(d, c):
        for side in range(2):

            @pl.when(sides[side][0])
            def _(side=side):
                halo(d, c, side).start()

    def split(h, c):
        for i in range(row_blocks):
            adj[h, c, i] = given[h, c * ROWS : (c + 1) * ROWS, i * 128 : (i + 1) * 128]

    for c in range(n_chunk):
        for d in range(1, n_harm):
            split(lax.rem(me_h + d, n_harm), c)
            arrive(d, c).start()
        split(me_h, c)
        own[c].start()
        start_halo(0, c)
        if c == 0:
            for load in loads:
                load.start()

    for load in small:
        load.wait()

    zone_row = lax.broadcasted_iota(jnp.int32, (128, WIDTH), 0)

    def select_step(i, carry):
        at = pl.ds(pl.multiple_of(i * WIDTH, WIDTH), WIDTH)
        hit = zone_row == (zone[:, at] - (pos - 1) * ZONE_DEV)
        w = weight[:, at]
        high = w.astype(jnp.bfloat16).astype(jnp.float32)
        select[0:128, at] = jnp.where(hit, high, 0.0).astype(jnp.bfloat16)
        select[128:256, at] = jnp.where(hit, w - high, 0.0).astype(jnp.bfloat16)
        return carry

    lax.fori_loop(0, nodes // WIDTH, select_step, 0)

    def block_of(c, index):
        return jnp.concatenate([ext[c][h, index] for h in range(n_harm)], axis=0)

    group = nodes // GROUPS
    half = chunk_rows // 2

    def back(d, c, q):
        peer = lax.rem(me_h + d, n_harm)
        return pltpu.make_async_remote_copy(
            src_ref=upd.at[peer, c, :, pl.ds(q * group, group)],
            dst_ref=ret.at[me_h, c, :, pl.ds(q * group, group)],
            send_sem=out_send.at[d, c, q],
            recv_sem=out_recv.at[d, c, q],
            device_id=(peer, me_n),
            device_id_type=MESH,
        )

    def own_back(c, q):
        return pltpu.make_async_copy(
            upd.at[me_h, c, :, pl.ds(q * group, group)],
            ret.at[me_h, c, :, pl.ds(q * group, group)],
            own_sem.at[c, q],
        )

    def start_back(c, q):
        for d in range(1, n_harm):
            back(d, c, q).start()
        own_back(c, q).start()

    def wait_halo(c):
        for side in range(2):

            @pl.when(sides[1 - side][0])
            def _(side=side):
                for d in range(n_harm):
                    halo(d, c, side).wait_recv()

    def conduct(c, start):
        results = []
        for u in range(UNROLL):
            b = start + u
            at = pl.ds(pl.multiple_of(b * 128, 128), 128)
            lam = block_of(c, row_blocks + b)
            taken = [lam]
            for s in range(1, blk.shape[1]):
                col = cols[s, b] - (pos - 1) * row_blocks
                col = jnp.minimum(jnp.maximum(col, 0), 3 * row_blocks - 1)
                taken.append(block_of(c, col))
            conduction = lax.dot_general(
                jnp.concatenate(taken, axis=1),
                jnp.concatenate([blk[b, s] for s in range(blk.shape[1])], axis=1),
                NT,
                preferred_element_type=jnp.float32,
            )
            residual = src[:, c, :, at].reshape(chunk_rows, 128) - conduction
            results.append((at, lam.astype(jnp.float32) + inv_diag[:, at] * residual))
        for at, result in results:
            upd[:, c, :, at] = result.reshape(n_harm, ROWS, 128).astype(jnp.bfloat16)

    for c in range(n_chunk):
        own[c].wait()
        for d in range(1, n_harm):
            arrive(d, c).wait_recv()
            start_halo(d, c)
        if c == 0:
            for load in loads:
                load.wait()

    row = lax.broadcasted_iota(jnp.int32, (chunk_rows, WIDTH), 0)
    rate_k = []
    for c in range(n_chunk):
        natural = (row // ROWS) * (n_chunk * ROWS) + c * ROWS + row % ROWS
        middle = n_chunk * n_harm * ROWS // 2
        rate_k.append(jnp.where(natural < middle, natural, middle - natural).astype(jnp.float32))

    def local_step(i, carry):
        at = pl.ds(pl.multiple_of(i * WIDTH, WIDTH), WIDTH)
        first = row_blocks + i * (WIDTH // 128)
        pieces = [
            jnp.concatenate([block_of(c, first + t) for t in range(WIDTH // 128)], axis=1)
            for c in range(n_chunk)
        ]
        field = jnp.concatenate(pieces, axis=0) if n_chunk > 1 else pieces[0]
        samples = jnp.dot(fourier[...], field, preferred_element_type=jnp.float32)
        weighted = (rad[:, at].astype(jnp.float32) * samples).astype(jnp.bfloat16)
        radiative = jnp.dot(fourier_t[...], weighted, preferred_element_type=jnp.float32)
        cap = capacity[:, at]
        for c in range(n_chunk):
            lam = pieces[c].astype(jnp.float32)
            swapped = jnp.concatenate([lam[half:], lam[:half]], axis=0)
            rows = slice(c * chunk_rows, (c + 1) * chunk_rows)
            rate = rate_k[c] * swapped
            rest = src[:, c, :, at].reshape(chunk_rows, WIDTH) - (cap * rate + radiative[rows])
            src[:, c, :, at] = rest.reshape(n_harm, ROWS, WIDTH)
        return carry

    lax.fori_loop(0, nodes // WIDTH, local_step, 0)

    group_steps = group // 128 // UNROLL
    for c in range(n_chunk):
        wait_halo(c)
        for q in range(GROUPS):

            def final_step(i, carry, c=c):
                conduct(c, i * UNROLL)
                return carry

            lax.fori_loop(q * group_steps, (q + 1) * group_steps, final_step, 0)
            start_back(c, q)

    part[...] = jnp.zeros_like(part)

    def gradient_step(i, carry):
        at = pl.ds(pl.multiple_of(i * 512, 512), 512)
        new = upd[:, :, :, at].reshape(n_chunk * chunk_rows, 512)
        both = lax.dot_general(select[:, at], new, NT, preferred_element_type=jnp.float32)
        part[...] += both[0:128] + both[128:256]
        return carry

    lax.fori_loop(0, nodes // 512, gradient_step, 0)

    def hand_over(side):
        _, device, place = sides[side]
        rows = pl.ds(0 if side == 0 else 2 * ZONE_DEV, ZONE_DEV)
        return pltpu.make_async_remote_copy(
            src_ref=part.at[rows, :],
            dst_ref=from_next if side == 0 else from_prev,
            send_sem=part_send.at[side],
            recv_sem=part_recv.at[side],
            device_id=device,
            device_id_type=MESH,
        )

    for side in range(2):

        @pl.when(sides[side][0])
        def _(side=side):
            hand_over(side).start()

    grad[...] = part[ZONE_DEV : 2 * ZONE_DEV, :]

    for side, buffer in ((0, from_next), (1, from_prev)):

        @pl.when(sides[1 - side][0])
        def _(side=side, buffer=buffer):
            hand_over(side).wait_recv()
            grad[...] += buffer[...]

    for c in range(n_chunk):
        for q in range(GROUPS):
            own_back(c, q).wait()
            for d in range(1, n_harm):
                back(d, c, q).wait()
        for d in range(1, n_harm):
            arrive(d, c).wait_send()
    for side in range(2):

        @pl.when(sides[side][0])
        def _(side=side):
            hand_over(side).wait_send()
            for c in range(n_chunk):
                for d in range(n_harm):
                    halo(d, c, side).wait_send()


def body(
    n_harm,
    n_node,
    adjoint,
    source,
    rad_coeff,
    capacity,
    inv_diag,
    blocks,
    block_cols,
    zone_of,
    heater_weight,
):
    rows, _, nodes = adjoint.shape
    n_chunk = rows // ROWS
    harmonics = n_harm * rows
    order = np.arange(harmonics).reshape(n_harm, n_chunk, ROWS).transpose(1, 0, 2).reshape(-1)
    basis = fourier_basis(harmonics)

    row_blocks = nodes // 128
    sent = adjoint.transpose(1, 0, 2)
    vmem = pl.BlockSpec(memory_space=pltpu.VMEM)
    smem = pl.BlockSpec(memory_space=pltpu.SMEM)
    hbm = pl.BlockSpec(memory_space=pltpu.HBM)
    piece = (n_harm, n_chunk, ROWS, nodes)
    dma = pltpu.SemaphoreType.DMA
    returned, gradient = pl.pallas_call(
        functools.partial(kernel, n_harm, n_node, n_chunk),
        out_shape=(
            jax.ShapeDtypeStruct(piece, jnp.bfloat16),
            jax.ShapeDtypeStruct((ZONE_DEV, harmonics), jnp.float32),
        ),
        in_specs=[vmem] + [hbm] * 7 + [smem, hbm, hbm],
        out_specs=(vmem, vmem),
        scratch_shapes=[pltpu.VMEM((n_harm, 3 * row_blocks, ROWS, 128), jnp.bfloat16)] * n_chunk
        + [
            pltpu.VMEM((1, nodes), jnp.float32),
            pltpu.VMEM((1, nodes), jnp.float32),
            pltpu.VMEM((1, nodes), jnp.float32),
            pltpu.VMEM((1, nodes), jnp.int32),
            pltpu.VMEM((harmonics, harmonics), jnp.bfloat16),
            pltpu.VMEM((harmonics, harmonics), jnp.bfloat16),
            pltpu.VMEM((n_harm, n_chunk, row_blocks, ROWS, 128), jnp.bfloat16),
            pltpu.VMEM(piece, jnp.float32),
            pltpu.VMEM(rad_coeff.shape, jnp.bfloat16),
            pltpu.VMEM(blocks.shape, jnp.bfloat16),
            pltpu.VMEM(piece, jnp.bfloat16),
            pltpu.VMEM((256, nodes), jnp.bfloat16),
            pltpu.VMEM((128, harmonics), jnp.float32),
            pltpu.VMEM((ZONE_DEV, harmonics), jnp.float32),
            pltpu.VMEM((ZONE_DEV, harmonics), jnp.float32),
            dma((3 + n_chunk,)),
            dma((n_harm, n_chunk)),
            dma((n_harm, n_chunk)),
            dma((2, n_harm, n_chunk)),
            dma((2, n_harm, n_chunk)),
            dma((n_harm, n_chunk, GROUPS)),
            dma((n_harm, n_chunk, GROUPS)),
            dma((n_chunk, GROUPS)),
            dma((2,)),
            dma((2,)),
            dma((6,)),
        ],
        compiler_params=pltpu.CompilerParams(
            collective_id=0, has_side_effects=True, vmem_limit_bytes=48 * 2**20
        ),
    )(
        sent,
        source.reshape(piece),
        rad_coeff,
        blocks,
        capacity[None, :],
        inv_diag[None, :],
        heater_weight[None, :],
        zone_of[None, :],
        block_cols.T,
        jnp.asarray(basis[:, order]),
        jnp.asarray(basis.T[order]),
    )
    return returned.reshape(n_harm, rows, nodes).transpose(1, 0, 2), gradient


def solution(mesh):
    in_specs = (
        P("harm", None, "node"),
        P(None, ("harm", "node")),
        P(None, ("harm", "node")),
        P(("harm", "node")),
        P(("harm", "node")),
        P(("harm", "node"), None, None, None),
        P(("harm", "node"), None),
        P(("harm", "node")),
        P(("harm", "node")),
    )
    out_specs = (P("harm", None, "node"), P(("harm", "node"), None))
    step = functools.partial(body, mesh.shape["harm"], mesh.shape["node"])
    return jax.shard_map(step, mesh=mesh, in_specs=in_specs, out_specs=out_specs, check_vma=False)
```
